32 devices in a mesh: dp: 4 (over y, core), seq: 8 (over z, x).
Axes of the slice: x: 2, y: 2, z: 4, core: 2. Of those that a mesh axis runs over, the one named last changes fastest.
Arguments:
- hidden: bfloat16 [4096, 2048], P(('dp', 'seq')), may hold values from -6 to 6
- queries: bfloat16 [4096, 2048], P(('dp', 'seq')), may hold values from -360 to 360
- values: bfloat16 [4096, 512], P(('dp', 'seq')), may hold values from -6 to 6
- row_target: int32 [4096], P(('dp', 'seq')), may hold values from 0 to 1023, as said below
- key_weight: bfloat16 [2048, 512], P(('dp', 'seq')), may hold values from -0.125 to 0.125
- dialogue_lengths: int32 [4, 16], P('dp'), may hold values from 1 to 256, 1024 in all within a row
- teacher_pick: int32 [4096, 128], P(('dp', 'seq')), may hold values from 0 to 65279
- teacher_prob: float32 [4096, 128], P(('dp', 'seq')), may hold values from 0.02 to 1
Outputs:
- attn_out: bfloat16 [4096, 2048], P(('dp', 'seq'))
- token_loss: float32 [4096], P(('dp', 'seq'))
- weight_grad: float32 [2048, 512], P(('dp', 'seq'))
The draws below stay inside these ranges and needn't reach their ends.
Inputs may be any that keep to these rules, and one draw needn't show every extreme that they name: Within each pack, row_target holds every position 0 to 1023 once. Of the 128 rows of one device, at most 24 have targets in one block of 128 positions (target // 128 names the block), and in every draw some device sends exactly 24 to some block.
All inputs are finite; a program needn't handle non-finite values.
Results may differ from the reference program's by a relative error of at most 0.012.
The reference program's roundings to bfloat16 on the way count: a program that leaves them out, or rounds other values in their place, can miss the bound.
Values may be sent and summed in bfloat16 or wider, within the bound.
A program may use at most 64 MiB of HBM per device.

```python
import math
import jax
import jax.numpy as jnp
import numpy as np
from jax import lax

D = 2048
HEADS = 16
KV_HEADS = 4
HEAD_DIM = 128
TOPK = 8
SPAN = 2
TOK_DEV = 128
PACK = 1024
TOKENS = 4096
MOST = 256
NDIAL = 16
N_DP = 4
N_SEQ = 8


def shuffle_entries(entries, shuffle_key):
    return entries[jax.random.permutation(shuffle_key, entries.shape[0])]


def pack_targets(pack_key):
    per_shard = TOK_DEV // N_SEQ
    halfway = per_shard // 2
    pair_count = N_SEQ // 2
    sub_keys = jax.random.split(pack_key, 5)
    moves = jax.random.randint(sub_keys[0], (pair_count,), -halfway, halfway + 1)
    moves = moves.at[0].set(halfway)
    shares = jnp.concatenate([per_shard + moves, per_shard - moves]).astype(jnp.int32)
    shares = shares[jax.random.permutation(sub_keys[1], N_SEQ)]
    left_order = jax.random.permutation(sub_keys[2], N_SEQ)
    right_order = jax.random.permutation(sub_keys[3], N_SEQ)
    counts = shares[(right_order[None, :] - left_order[:, None]) % N_SEQ]
    earlier = (jnp.cumsum(counts, axis=0) - counts).astype(jnp.int32)
    upto = jnp.cumsum(counts, axis=1).astype(jnp.int32)
    lower = upto - counts
    ordinal = jnp.arange(TOK_DEV, dtype=jnp.int32)
    shard_of = jnp.sum((upto[:, None, :] <= ordinal[None, :, None]).astype(jnp.int32), axis=2)
    within = ordinal[None, :] - jnp.take_along_axis(lower, shard_of, axis=1)
    target = shard_of * TOK_DEV + jnp.take_along_axis(earlier, shard_of, axis=1) + within
    mix_keys = jax.random.split(sub_keys[4], N_SEQ)
    target = jax.vmap(shuffle_entries)(target, mix_keys)
    return target.reshape(PACK).astype(jnp.int32)


def draw_row_target(key, part):
    pack_keys = jax.random.split(jax.random.fold_in(key, 11), TOKENS // PACK)
    return jax.vmap(pack_targets)(pack_keys).reshape(TOKENS)


def draw_queries(key, part):
    first_key = jax.random.fold_in(jax.random.fold_in(key, 23), 0)
    normal_part = jnp.clip(jax.random.normal(first_key, (TOKENS, HEADS * HEAD_DIM), jnp.float32), -6.0, 6.0)
    return normal_part.astype(jnp.bfloat16)


def with_ends(values, stream_key, smallest, largest):
    longest = values.shape.index(max(values.shape))
    spots = []
    for shift in (0, 1):
        where = [jax.random.randint(jax.random.fold_in(stream_key, axis), (), 0, length) for axis, length in enumerate(values.shape)]
        where[longest] = (where[longest] + shift) % values.shape[longest]
        spots.append(tuple(where))
    return values.at[spots[0]].set(smallest).at[spots[1]].set(largest)


def shard_levels(own_key, shape, shards, low, top_value):
    def one(position, parts):
        heights = jax.random.uniform(jax.random.fold_in(jax.random.fold_in(own_key, 6), position), (parts,), jnp.float32, low / len(shards), top_value / len(shards))
        return jnp.repeat(jnp.exp(heights), shape[position] // parts).reshape((-1,) + (1,) * (len(shape) - position - 1))

    gain = one(*shards[0])
    for cut in shards[1:]:
        gain = gain * one(*cut)
    return gain


def split_up(count, total, bound, skew):
    portions = [(1 << 20) // math.isqrt(standing ** skew) + 1 for standing in range(2, count + 1)]
    spare, given = total - bound - (count - 1), [1] * (count - 1)
    while spare > 0:
        movable = [i for i in range(count - 1) if given[i] < bound]
        pool, budget = sum([portions[i] for i in movable]), spare
        for i in movable:
            addition = min(bound - given[i], max(1, budget * portions[i] // pool), spare)
            given[i] = given[i] + addition
            spare = spare - addition
    return np.array([bound] + given)


def ragged_sizes(rng, amount, total, limit, lean):
    if amount == 2:
        one = jax.random.randint(rng, (), max(1, total - limit), min(limit, total - 1) + 1)
        return jnp.stack([one, total - one])
    sizes = jnp.asarray(split_up(amount, total, limit, lean), jnp.int32)
    couples = (amount - 1) // 2
    donor, taker = sizes[1:1 + 2 * couples:2], sizes[2:2 + 2 * couples:2]
    margin = jnp.minimum(donor - 1, limit - taker)
    moved = jax.random.randint(jax.random.fold_in(rng, 1), (couples,), 0, 1 << 20) % (margin + 1)
    sizes = sizes.at[1:1 + 2 * couples:2].set(donor - moved).at[2:2 + 2 * couples:2].set(taker + moved)
    return sizes[jax.random.permutation(jax.random.fold_in(rng, 2), amount)]


def gaussian(stream_key, extent, scale, limit, cuts=(), kind=jnp.bfloat16):
    values = jax.random.normal(stream_key, extent, jnp.float32) * scale
    if len(cuts) > 0:
        values = shard_levels(stream_key, extent, cuts, -0.22, 0.18) * values
    return jnp.clip(values, min=-limit, max=limit).astype(kind)


def setup_inputs(seed: int = 0) -> dict:
    seeds = jax.random.split(jax.random.key(seed), 9)
    hidden = gaussian(seeds[0], (TOKENS, D), 1.0, 6.0, ((0, 32),))
    queries = draw_queries(jax.random.fold_in(seeds[8], 71), 0)
    values = gaussian(seeds[2], (TOKENS, KV_HEADS * HEAD_DIM), 1.0, 6.0, ((0, 32),))
    row_target = draw_row_target(jax.random.fold_in(seeds[8], 71), 0)
    key_weight = gaussian(seeds[4], (D, KV_HEADS * HEAD_DIM), D ** -0.5, 0.125, ((0, 32),))
    dialogue_lengths = jax.vmap(lambda own: ragged_sizes(own, NDIAL, PACK, MOST, 2))(jax.random.split(seeds[5], N_DP)).reshape((N_DP, NDIAL)).astype(jnp.int32)
    teacher_pick = with_ends(jax.random.randint(seeds[6], (TOKENS, HEADS * TOPK), 0, 65280), jax.random.fold_in(seeds[6], 1), 0, 65279).astype(jnp.int32)
    teacher_prob = jnp.clip(jnp.exp(math.log(1.0) - 3.912023 * jax.random.uniform(seeds[7], (TOKENS, HEADS * TOPK), jnp.float32) ** shard_levels(seeds[7], (TOKENS, HEADS * TOPK), ((0, 32),), -0.2, 0.2)), 0.02, 1.0)
    return dict(hidden=hidden, queries=queries, values=values, row_target=row_target, key_weight=key_weight, dialogue_lengths=dialogue_lengths, teacher_pick=teacher_pick, teacher_prob=teacher_prob)


negative = -1.0e30
rope_base = 500000.0


def rotate(matrix, positions, direction):
    count = matrix.shape[0]
    split = matrix.reshape(count, -1, HEAD_DIM)
    halfway = HEAD_DIM // 2
    frequency = rope_base ** (-2.0 * jnp.arange(halfway, dtype=jnp.float32) / HEAD_DIM)
    angle = positions.astype(jnp.float32)[:, None] * frequency[None, :]
    cosine = jnp.cos(angle)[:, None, :]
    sine = direction * jnp.sin(angle)[:, None, :]
    first_half = split[..., :halfway]
    second_half = split[..., halfway:]
    joined = jnp.concatenate([first_half * cosine - second_half * sine, second_half * cosine + first_half * sine], axis=-1)
    return joined.reshape(count, -1)


def dialogue_starts(lengths, positions):
    ending = jnp.cumsum(lengths).astype(jnp.int32)
    picked = jnp.where(ending[None, :] <= positions[:, None], lengths[None, :], 0)
    return jnp.sum(picked, axis=1).astype(jnp.int32)


def block_targets(label_index, label_prob, key_start, width, head_count):
    row_count = label_index.shape[0]
    within = label_index - key_start
    within = jnp.where((within >= 0) & (within < width), within, width).astype(jnp.int32)
    head_ids = jnp.broadcast_to(jnp.arange(head_count, dtype=jnp.int32)[None, :, None], label_index.shape)
    row_ids = jnp.broadcast_to(jnp.arange(row_count, dtype=jnp.int32)[:, None, None], label_index.shape)
    table = jnp.zeros((head_count, row_count, width), jnp.float32)
    return table.at[head_ids, row_ids, within].add(label_prob, mode="drop")


def reference(hidden, queries, values, row_target, key_weight, dialogue_lengths, teacher_pick, teacher_prob):
    pack_count = TOKENS // PACK
    group_size = HEADS // KV_HEADS
    kv_width = KV_HEADS * HEAD_DIM
    padding = SPAN * TOK_DEV
    window = padding + TOK_DEV
    scaling = HEAD_DIM ** -0.5

    def one_pack(item):
        hidden_in, queries_in, values_in, target_in, lengths, pick_in, prob_in = item
        hidden_seq = jnp.zeros((PACK, D), jnp.bfloat16).at[target_in].set(hidden_in)
        queries_seq = jnp.zeros((PACK, HEADS * HEAD_DIM), jnp.bfloat16).at[target_in].set(queries_in)
        values_seq = jnp.zeros((PACK, kv_width), jnp.bfloat16).at[target_in].set(values_in)
        positions = jnp.arange(PACK, dtype=jnp.int32)
        starts = dialogue_starts(lengths, positions)
        projected = jnp.dot(hidden_seq, key_weight, preferred_element_type=jnp.float32)
        keys_seq = rotate(projected, positions, 1.0).astype(jnp.bfloat16)
        keys_pad = jnp.concatenate([jnp.zeros((padding, kv_width), jnp.bfloat16), keys_seq], axis=0)
        values_pad = jnp.concatenate([jnp.zeros((padding, kv_width), jnp.bfloat16), values_seq], axis=0)

        def block(carry, number):
            first_row = (number * TOK_DEV).astype(jnp.int32)
            query_pos = first_row + jnp.arange(TOK_DEV, dtype=jnp.int32)
            query_block = lax.dynamic_slice_in_dim(queries_seq, first_row, TOK_DEV, 0)
            query_start = lax.dynamic_slice_in_dim(starts, first_row, TOK_DEV, 0)
            key_block = lax.dynamic_slice_in_dim(keys_pad, first_row, window, 0)
            value_block = lax.dynamic_slice_in_dim(values_pad, first_row, window, 0)
            key_pos = first_row - padding + jnp.arange(window, dtype=jnp.int32)
            pick_block = lax.dynamic_slice_in_dim(pick_in, first_row, TOK_DEV, 0)
            prob_block = lax.dynamic_slice_in_dim(prob_in, first_row, TOK_DEV, 0).reshape(TOK_DEV, HEADS, TOPK)
            reach = (query_pos - query_start + 1)[:, None]
            label_index = (query_start[:, None] + pick_block % reach).reshape(TOK_DEV, HEADS, TOPK).astype(jnp.int32)
            query_heads = query_block.reshape(TOK_DEV, KV_HEADS, group_size, HEAD_DIM).astype(jnp.float32)
            key_heads = key_block.reshape(window, KV_HEADS, HEAD_DIM).astype(jnp.float32)
            value_heads = value_block.reshape(window, KV_HEADS, HEAD_DIM).astype(jnp.float32)
            score = jnp.einsum("tkgd,wkd->kgtw", query_heads, key_heads) * scaling
            allowed = (key_pos[None, :] >= query_start[:, None]) & (key_pos[None, :] <= query_pos[:, None])
            held = jnp.where(allowed[None, None], score, negative)
            top_score = jnp.max(held, axis=-1)
            lse = top_score + jnp.log(jnp.sum(jnp.exp(held - top_score[..., None]), axis=-1))
            weight = jnp.exp(held - lse[..., None])
            table = block_targets(label_index, prob_block, first_row - padding, window, HEADS)
            table = table.reshape(KV_HEADS, group_size, TOK_DEV, window)
            mass = jnp.sum(prob_block, axis=2).T.reshape(KV_HEADS, group_size, TOK_DEV)
            entropy = jnp.sum(prob_block * jnp.log(prob_block), axis=(1, 2))
            picked = jnp.sum(table * score, axis=(0, 1, 3))
            loss = (entropy - picked + jnp.sum(mass * lse, axis=(0, 1))) / HEADS
            rounded = weight.astype(jnp.bfloat16).astype(jnp.float32)
            output = jnp.einsum("kgtw,wkd->tkgd", rounded, value_heads).astype(jnp.bfloat16)
            output = output.reshape(TOK_DEV, HEADS * HEAD_DIM)
            slope = ((weight * mass[..., None] - table) / HEADS).astype(jnp.bfloat16).astype(jnp.float32)
            gradient = jnp.einsum("kgtw,tkgd->wkd", slope, query_heads) * scaling
            gradient = gradient.reshape(window, kv_width)
            current = lax.dynamic_slice_in_dim(carry, first_row, window, 0)
            carry = lax.dynamic_update_slice_in_dim(carry, current + gradient, first_row, 0)
            return carry, (output, loss)

        initial = jnp.zeros((PACK + padding, kv_width), jnp.float32)
        grads_pad, (outputs, losses) = lax.scan(block, initial, jnp.arange(N_SEQ, dtype=jnp.int32))
        key_grad = rotate(grads_pad[padding:], positions, -1.0).astype(jnp.bfloat16)
        term = jnp.dot(hidden_seq.T, key_grad, preferred_element_type=jnp.float32)
        return outputs.reshape(PACK, HEADS * HEAD_DIM), losses.reshape(PACK), term

    items = (
        hidden.reshape(pack_count, PACK, D),
        queries.reshape(pack_count, PACK, HEADS * HEAD_DIM),
        values.reshape(pack_count, PACK, kv_width),
        row_target.reshape(pack_count, PACK),
        dialogue_lengths,
        teacher_pick.reshape(pack_count, PACK, HEADS * TOPK),
        teacher_prob.reshape(pack_count, PACK, HEADS * TOPK),
    )
    outputs, losses, terms = lax.map(one_pack, items)
    weight_grad = jnp.sum(terms, axis=0) * (TOKENS ** -0.5)
    return outputs.reshape(TOKENS, HEADS * HEAD_DIM), losses.reshape(TOKENS), weight_grad
```

```python
import functools

import jax
import jax.numpy as jnp
from jax import lax
from jax.experimental import pallas as pl
from jax.experimental.pallas import tpu as pltpu
from jax.sharding import PartitionSpec as P

HEAD_DIM = 128
SPAN = 2
MESH = pl.DeviceIdType.MESH
VMEM_BYTES = 50 * 1024 * 1024

negative = -1e30
rope_base = 500000.0


def angles(positions):
    halfway = HEAD_DIM // 2
    frequency = rope_base ** (-2.0 * jnp.arange(halfway, dtype=jnp.float32) / HEAD_DIM)
    angle = positions.astype(jnp.float32)[:, None] * frequency[None, :]
    cosine = jnp.cos(angle)
    sine = jnp.sin(angle)
    return (
        jnp.concatenate([cosine, cosine], axis=1),
        jnp.concatenate([-sine, sine], axis=1),
    )


def turned(block, cosine, sine):
    return block * cosine + pltpu.roll(block, HEAD_DIM // 2, 1) * sine


def dot(a, b, ca=1, cb=0):
    return lax.dot_general(a, b, (((ca,), (cb,)), ((), ())), preferred_element_type=jnp.float32)


def greet(seq_n, dp_n):
    s = lax.axis_index("seq")
    p = lax.axis_index("dp")
    barrier = pltpu.get_barrier_semaphore()
    for k in range(1, seq_n):
        pl.semaphore_signal(
            barrier, inc=1, device_id=(p, lax.rem(s + k, seq_n)), device_id_type=MESH
        )
    for k in range(1, dp_n):
        pl.semaphore_signal(
            barrier, inc=1, device_id=(lax.rem(p + k, dp_n), s), device_id_type=MESH
        )
    pl.semaphore_wait(barrier, seq_n - 1 + dp_n - 1)


def remote(src, dst, send, recv, p, s):
    return pltpu.make_async_remote_copy(
        src_ref=src, dst_ref=dst, send_sem=send, recv_sem=recv, device_id=(p, s),
        device_id_type=MESH,
    )


def gather_kernel(
    seq_n, dp_n, inside,
    w_ref, hidden_ref, query_ref, value_ref, left_ref, right_ref, spot_ref, cos_ref, sin_ref,
    cols_ref, target_ref,
    q_out, kv_out, cols_out, target_out,
    wall, parcel, got, kparcel, kgot,
    wz_s, wz_r, wx_s, wx_r, wy_s, wy_r, wc_s, wc_r,
    par_s, par_r, col_s, col_r, tgt_s, tgt_r, k_s, k_r, sh_s, sh_r,
):
    s = lax.axis_index("seq")
    p = lax.axis_index("dp")
    rows = query_ref.shape[0]
    qhalf = query_ref.shape[1] // 2
    vhalf = value_ref.shape[1] // 2
    kvn = value_ref.shape[1] // HEAD_DIM
    heads = query_ref.shape[1] // HEAD_DIM
    group = heads // kvn
    slots = got.shape[1]
    cap = slots // 2
    greet(seq_n, dp_n)
    waits = []
    if inside:
        a, b = s // 2, lax.rem(s, 2)
        yb, cc = p // 2, lax.rem(p, 2)
        na, nb = seq_n // 2, dp_n // 2
        wall[p, s] = w_ref[...]
        zc = []
        for k in range(1, na):
            cp = remote(w_ref, wall.at[p, s], wz_s.at[k], wz_r.at[k], p, lax.rem(a + k, na) * 2 + b)
            cp.start()
            zc.append(cp)

    left = left_ref[...]
    right = right_ref[...]
    parcel[:, :, 0:qhalf] = (
        (dot(left, query_ref[:, 0:qhalf]) + dot(right, query_ref[:, qhalf:]))
        .astype(jnp.bfloat16).reshape(seq_n, slots, qhalf)
    )
    parcel[:, :, qhalf:qhalf + vhalf] = (
        (dot(left, value_ref[:, 0:vhalf]) + dot(right, value_ref[:, vhalf:]))
        .astype(jnp.bfloat16).reshape(seq_n, slots, vhalf)
    )
    parcel[:, :, qhalf + vhalf:] = (
        dot(left + right, spot_ref[...]).astype(jnp.bfloat16).reshape(seq_n, slots, rows)
    )
    par = []
    for k in range(1, seq_n):
        to = lax.rem(s + k, seq_n)
        cp = remote(parcel.at[to], got.at[s], par_s.at[k], par_r.at[k], p, to)
        cp.start()
        par.append(cp)
    got[s] = parcel[s]
    target_out[s] = target_ref[...]
    cols_out[s] = cols_ref[s]

    if inside:
        cores = []

        def to_core(y, sh, slot):
            cp = remote(
                wall.at[y * 2 + cc, sh], wall.at[y * 2 + cc, sh], wc_s.at[slot], wc_r.at[slot],
                yb * 2 + 1 - cc, s,
            )
            cp.start()
            cores.append(cp)

        ys = []

        def to_y(sh, slot):
            for m in range(1, nb):
                cp = remote(
                    wall.at[p, sh], wall.at[p, sh], wy_s.at[m, slot], wy_r.at[m, slot],
                    lax.rem(yb + m, nb) * 2 + cc, s,
                )
                cp.start()
                ys.append((cp, m, slot))
            to_core(yb, sh, slot)

        xs = []
        for k in range(na):
            if k > 0:
                zc[k - 1].wait_recv()
            sh = lax.rem(a - k + na, na) * 2 + b
            cp = remote(wall.at[p, sh], wall.at[p, sh], wx_s.at[k], wx_r.at[k], p, a * 2 + 1 - b)
            cp.start()
            xs.append(cp)
            to_y(sh, 2 * k)
        for k in range(na):
            xs[k].wait_recv()
            to_y(lax.rem(a - k + na, na) * 2 + 1 - b, 2 * k + 1)
        for cp, m, slot in ys:
            cp.wait_recv()
            k, other = slot // 2, slot % 2
            sh = lax.rem(a - k + na, na) * 2 + (1 - b if other else b)
            to_core(lax.rem(yb - m + nb, nb), sh, m * seq_n + slot)
        for cp in cores:
            cp.wait_recv()
        waits += zc + xs + [c[0] for c in ys] + cores
        weights = wall[...].reshape(hidden_ref.shape[1], -1)
    else:
        weights = w_ref[...]

    projected = dot(hidden_ref[...], weights)
    cosine = cos_ref[...]
    sine = sin_ref[...]
    keys = jnp.concatenate(
        [
            turned(projected[:, g * HEAD_DIM:(g + 1) * HEAD_DIM], cosine, sine)
            for g in range(kvn)
        ],
        axis=1,
    ).astype(jnp.bfloat16)
    kparcel[...] = (
        (dot(left, keys[:, 0:vhalf]) + dot(right, keys[:, vhalf:]))
        .astype(jnp.bfloat16).reshape(seq_n, slots, vhalf)
    )
    ks = []
    for k in range(1, seq_n):
        to = lax.rem(s + k, seq_n)
        cp = remote(kparcel.at[to], kgot.at[s], k_s.at[k], k_r.at[k], p, to)
        cp.start()
        ks.append(cp)
    for k in range(1, seq_n):
        to = lax.rem(s + k, seq_n)
        cp = remote(cols_ref.at[to], cols_out.at[s], col_s.at[k], col_r.at[k], p, to)
        cp.start()
        waits.append(cp)
        cp = remote(target_ref, target_out.at[s], tgt_s.at[k], tgt_r.at[k], p, to)
        cp.start()
        waits.append(cp)
    kgot[s] = kparcel[s]

    for cp in par:
        cp.wait_recv()
    marks = got[:, :, qhalf + vhalf:].reshape(seq_n * slots, rows)
    place = lax.rem(lax.broadcasted_iota(jnp.int32, marks.shape, 0), slots)
    first = jnp.where(place < cap, marks, jnp.zeros_like(marks))
    second = jnp.where(place < cap, jnp.zeros_like(marks), marks)
    for half, mark in ((0, first), (1, second)):
        base = half * (heads // 2)
        settled = dot(mark, got[:, :, 0:qhalf].reshape(seq_n * slots, qhalf), 0, 0).astype(
            jnp.bfloat16
        )
        for h in range(heads // 2):
            head = base + h
            q_out[head // group, (head % group) * rows:(head % group + 1) * rows, :] = settled[
                :, h * HEAD_DIM:(h + 1) * HEAD_DIM
            ]
        settled = dot(
            mark, got[:, :, qhalf:qhalf + vhalf].reshape(seq_n * slots, vhalf), 0, 0
        ).astype(jnp.bfloat16)
        for h in range(kvn // 2):
            kv_out[kvn + half * (kvn // 2) + h, SPAN * rows:, :] = settled[
                :, h * HEAD_DIM:(h + 1) * HEAD_DIM
            ]
    for cp in ks:
        cp.wait_recv()
    for half, mark in ((0, first), (1, second)):
        settled = dot(mark, kgot[...].reshape(seq_n * slots, vhalf), 0, 0).astype(jnp.bfloat16)
        for h in range(kvn // 2):
            kv_out[half * (kvn // 2) + h, SPAN * rows:, :] = settled[
                :, h * HEAD_DIM:(h + 1) * HEAD_DIM
            ]

    def shift(by):
        return remote(
            kv_out.at[:, SPAN * rows:(SPAN + 1) * rows, :],
            kv_out.at[:, (SPAN - by) * rows:(SPAN - by + 1) * rows, :],
            sh_s.at[by], sh_r.at[by], p, lax.rem(s + by, seq_n),
        )

    for by in range(1, SPAN + 1):
        @pl.when(s + by < seq_n)
        def _(by=by):
            shift(by).start()

        @pl.when(s < by)
        def _(by=by):
            kv_out[:, (SPAN - by) * rows:(SPAN - by + 1) * rows, :] = jnp.zeros(
                (2 * kvn, rows, HEAD_DIM), jnp.bfloat16
            )
    for cp in par + ks:
        cp.wait_send()
    if inside:
        for cp in zc + xs + [c[0] for c in ys] + cores:
            cp.wait_send()
        waits = waits[len(zc) + len(xs) + len(ys) + len(cores):]
    for cp in waits:
        cp.wait()
    for by in range(1, SPAN + 1):
        @pl.when(s + by < seq_n)
        def _(by=by):
            shift(by).wait_send()

        @pl.when(s >= by)
        def _(by=by):
            shift(by).wait_recv()


def attention_kernel(
    head_total, q_ref, k_ref, v_ref, pick_ref, prob_ref, start_ref, out_ref, loss_ref, grad_ref
):
    step = pl.program_id(0)
    scaling = HEAD_DIM ** (-0.5)
    queries = q_ref[0]
    width = k_ref.shape[1]
    lanes = queries.shape[0]
    rows = out_ref.shape[0]
    group = lanes // rows
    score = dot(k_ref[0], queries, 1, 1) * scaling
    spot = lax.broadcasted_iota(jnp.int32, (width, lanes), 0)
    last = lax.rem(lax.broadcasted_iota(jnp.int32, (1, lanes), 1), rows) + (width - rows)
    allowed = (spot >= start_ref[...]) & (spot <= last)
    held = jnp.where(allowed, score, negative)
    top = jnp.max(held, axis=0, keepdims=True)
    raised = jnp.exp(held - top)
    total = jnp.sum(raised, axis=0, keepdims=True)
    lse = top + jnp.log(total)
    weight = raised * (1.0 / total)
    prob = prob_ref[0]
    table = jnp.zeros((width, lanes), jnp.float32)
    for k in range(prob.shape[0]):
        table += jnp.where(spot == pick_ref[0, k:k + 1, :], prob[k:k + 1, :], 0.0)
    mass = jnp.sum(prob, axis=0, keepdims=True)
    entropy = jnp.sum(prob * jnp.log(prob), axis=0, keepdims=True)
    picked = jnp.sum(table * score, axis=0, keepdims=True)
    loss = (entropy - picked + mass * lse) / head_total
    part = loss[:, 0:rows]
    for h in range(1, group):
        part += loss[:, h * rows:(h + 1) * rows]

    @pl.when(step == 0)
    def _():
        loss_ref[...] = part

    @pl.when(step > 0)
    def _():
        loss_ref[...] += part

    output = dot(weight.astype(jnp.bfloat16), v_ref[0], 0, 0).astype(jnp.bfloat16)
    for h in range(group):
        out_ref[:, h * HEAD_DIM:(h + 1) * HEAD_DIM] = output[h * rows:(h + 1) * rows, :]
    slope = ((weight * mass - table) * (1.0 / head_total)).astype(jnp.bfloat16)
    grad_ref[...] = dot(slope, queries) * scaling


def gradient_kernel(
    seq_n, dp_n, scale,
    grad_ref, cos_ref, sin_ref, cols_ref, target_ref,
    out_ref,
    sent, back, sorted_cols, kg, share, arrived,
    b_s, b_r, z_s, z_r, x_s, x_r, d_s, d_r,
):
    s = lax.axis_index("seq")
    p = lax.axis_index("dp")
    rows = cos_ref.shape[0]
    a, b = s // 2, lax.rem(s, 2)
    na = seq_n // 2
    greet(seq_n, dp_n)
    for by in range(1, SPAN + 1):
        sent[by - 1] = grad_ref[(SPAN - by) * rows:(SPAN - by + 1) * rows, :].astype(jnp.bfloat16)

    def shift(by):
        return remote(
            sent.at[by - 1], back.at[by - 1], b_s.at[by], b_r.at[by], p,
            lax.rem(s - by + seq_n, seq_n),
        )

    for by in range(1, SPAN + 1):
        @pl.when(s >= by)
        def _(by=by):
            shift(by).start()

        @pl.when(s + by >= seq_n)
        def _(by=by):
            back[by - 1] = jnp.zeros(back.shape[1:], jnp.bfloat16)

    count = seq_n * rows
    total = jnp.zeros((count, cols_ref.shape[2]), jnp.float32)
    spot = lax.broadcasted_iota(jnp.int32, (count, rows), 0)
    for j in range(seq_n):
        hit = jnp.where(spot == target_ref[j, 0:1, :], 1.0, 0.0).astype(jnp.bfloat16)
        total += dot(hit, cols_ref[j])
    sorted_cols[...] = total.astype(jnp.bfloat16).reshape(sorted_cols.shape)

    for by in range(1, SPAN + 1):
        @pl.when(s + by < seq_n)
        def _(by=by):
            shift(by).wait_recv()
    rotated = grad_ref[SPAN * rows:, :]
    for by in range(1, SPAN + 1):
        rotated += back[by - 1].astype(jnp.float32)
    cosine = cos_ref[...]
    sine = -sin_ref[...]
    kg[s] = jnp.concatenate(
        [
            turned(rotated[:, g * HEAD_DIM:(g + 1) * HEAD_DIM], cosine, sine)
            for g in range(rotated.shape[1] // HEAD_DIM)
        ],
        axis=1,
    ).astype(jnp.bfloat16)
    zc, xs = [], []
    for k in range(1, na):
        cp = remote(kg.at[s], kg.at[s], z_s.at[k], z_r.at[k], p, lax.rem(a + k, na) * 2 + b)
        cp.start()
        zc.append(cp)
    result = None
    for k in range(na):
        if k > 0:
            zc[k - 1].wait_recv()
        sh = lax.rem(a - k + na, na) * 2 + b
        cp = remote(kg.at[sh], kg.at[sh], x_s.at[k], x_r.at[k], p, a * 2 + 1 - b)
        cp.start()
        xs.append(cp)
        term = dot(sorted_cols[sh], kg[sh], 0, 0)
        result = term if result is None else result + term
    for k in range(na):
        xs[k].wait_recv()
        sh = lax.rem(a - k + na, na) * 2 + 1 - b
        result += dot(sorted_cols[sh], kg[sh], 0, 0)
    result *= scale
    depth = share.shape[1]
    for m in range(dp_n):
        share[m] = result[m * depth:(m + 1) * depth, :].astype(share.dtype)
    ds = []
    for m in range(1, dp_n):
        to = lax.rem(p + m, dp_n)
        cp = remote(share.at[to], arrived.at[m], d_s.at[m], d_r.at[m], to, s)
        cp.start()
        ds.append(cp)
    final = share[p].astype(jnp.float32)
    for m in range(1, dp_n):
        ds[m - 1].wait_recv()
        final += arrived[m].astype(jnp.float32)
    out_ref[...] = final
    for cp in zc + xs + ds:
        cp.wait_send()
    for by in range(1, SPAN + 1):
        @pl.when(s >= by)
        def _(by=by):
            shift(by).wait_send()


def local(
    hidden, queries, values, row_target, key_weight, dialogue_lengths, teacher_pick, teacher_prob
):
    rows = hidden.shape[0]
    seq_n = lax.axis_size("seq")
    dp_n = lax.axis_size("dp")
    s = lax.axis_index("seq")
    depth, kv_width = key_weight.shape
    capacity = rows // seq_n + rows // (2 * seq_n)
    capacity = -(-capacity // 8) * 8
    heads = queries.shape[1] // HEAD_DIM
    kvn = kv_width // HEAD_DIM
    group = heads // kvn
    top = teacher_pick.shape[1] // heads
    slots = 2 * capacity
    vmem = pl.BlockSpec(memory_space=pltpu.VMEM)
    dma = pltpu.SemaphoreType.DMA
    bf16 = jnp.bfloat16

    destination = row_target // rows
    offset = row_target - destination * rows
    order = jnp.arange(rows, dtype=jnp.int32)
    earlier = (destination[None, :] == destination[:, None]) & (order[None, :] < order[:, None])
    rank = jnp.sum(earlier.astype(jnp.int32), axis=1)
    slot = destination * slots + rank
    every = jnp.arange(seq_n * slots, dtype=jnp.int32)[:, None]
    left = (every == slot[None, :]).astype(bf16)
    right = (every == slot[None, :] + capacity).astype(bf16)
    marks = (offset[:, None] == order[None, :]).astype(bf16)
    cos_row, sin_row = angles(row_target)
    columns = hidden.reshape(rows, dp_n, seq_n, depth).transpose(2, 0, 1, 3)
    columns = columns.reshape(seq_n, rows, dp_n * depth)
    target_tile = jnp.broadcast_to(row_target[None, :], (8, rows))

    inside = depth % 16 == 0
    weight_in = key_weight
    if not inside:
        weight_in = lax.all_gather(key_weight, ("dp", "seq"), axis=0, tiled=True)
    qhalf, vhalf = queries.shape[1] // 2, kv_width // 2
    na, nb = seq_n // 2, dp_n // 2
    wall = (dp_n, seq_n, depth, kv_width) if inside else (8, 128)
    pairs = [
        (na,), (na,), (na,), (na,), (nb, seq_n), (nb, seq_n), (nb * seq_n,), (nb * seq_n,),
    ] + [(seq_n,)] * 8 + [(SPAN + 1,)] * 2
    q_seq, kv_win, cols_all, target_all = pl.pallas_call(
        functools.partial(gather_kernel, seq_n, dp_n, inside),
        out_shape=(
            jax.ShapeDtypeStruct((kvn, group * rows, HEAD_DIM), bf16),
            jax.ShapeDtypeStruct((2 * kvn, (SPAN + 1) * rows, HEAD_DIM), bf16),
            jax.ShapeDtypeStruct(columns.shape, bf16),
            jax.ShapeDtypeStruct((seq_n, 8, rows), jnp.int32),
        ),
        in_specs=[vmem] * 11,
        out_specs=(vmem,) * 4,
        scratch_shapes=[
            pltpu.VMEM(wall, bf16),
            pltpu.VMEM((seq_n, slots, qhalf + vhalf + rows), bf16),
            pltpu.VMEM((seq_n, slots, qhalf + vhalf + rows), bf16),
            pltpu.VMEM((seq_n, slots, vhalf), bf16),
            pltpu.VMEM((seq_n, slots, vhalf), bf16),
        ] + [dma(shape) for shape in pairs],
        compiler_params=pltpu.CompilerParams(
            collective_id=0, has_side_effects=True, vmem_limit_bytes=VMEM_BYTES
        ),
    )(
        weight_in, hidden, queries, values, left, right, marks, cos_row, sin_row, columns,
        target_tile,
    )

    positions = s * rows + order
    ending = jnp.cumsum(dialogue_lengths[0])
    starts = jnp.sum(
        jnp.where(ending[None, :] <= positions[:, None], dialogue_lengths[0][None, :], 0), axis=1
    )
    base = (s - SPAN) * rows
    reach = (positions - starts + 1)[:, None]
    picks = (starts[:, None] - base + teacher_pick % reach).reshape(rows, kvn, group, top)
    picks = picks.transpose(1, 3, 2, 0).reshape(kvn, top, group * rows)
    probs = teacher_prob.reshape(rows, kvn, group, top).transpose(1, 3, 2, 0)
    probs = probs.reshape(kvn, top, group * rows)
    lower = jnp.tile(starts - base, group)[None, :]
    width = (SPAN + 1) * rows
    lanes = group * rows
    attn_out, loss, grads = pl.pallas_call(
        functools.partial(attention_kernel, heads),
        grid=(kvn,),
        out_shape=(
            jax.ShapeDtypeStruct((rows, heads * HEAD_DIM), bf16),
            jax.ShapeDtypeStruct((1, rows), jnp.float32),
            jax.ShapeDtypeStruct((width, kv_width), jnp.float32),
        ),
        in_specs=[
            pl.BlockSpec((1, lanes, HEAD_DIM), lambda g: (g, 0, 0)),
            pl.BlockSpec((1, width, HEAD_DIM), lambda g: (g, 0, 0)),
            pl.BlockSpec((1, width, HEAD_DIM), lambda g: (g + kvn, 0, 0)),
            pl.BlockSpec((1, top, lanes), lambda g: (g, 0, 0)),
            pl.BlockSpec((1, top, lanes), lambda g: (g, 0, 0)),
            pl.BlockSpec((1, lanes), lambda g: (0, 0)),
        ],
        out_specs=(
            pl.BlockSpec((rows, group * HEAD_DIM), lambda g: (0, g)),
            pl.BlockSpec((1, rows), lambda g: (0, 0)),
            pl.BlockSpec((width, HEAD_DIM), lambda g: (0, g)),
        ),
        compiler_params=pltpu.CompilerParams(vmem_limit_bytes=VMEM_BYTES),
    )(q_seq, kv_win, kv_win, picks, probs, lower)

    cos_pos, sin_pos = angles(positions)
    link = bf16 if depth % 16 == 0 else jnp.float32
    weight_grad = pl.pallas_call(
        functools.partial(
            gradient_kernel, seq_n, dp_n, (rows * seq_n * dp_n) ** (-0.5)
        ),
        out_shape=jax.ShapeDtypeStruct((depth, kv_width), jnp.float32),
        in_specs=[vmem] * 5,
        out_specs=vmem,
        scratch_shapes=[
            pltpu.VMEM((SPAN, rows, kv_width), bf16),
            pltpu.VMEM((SPAN, rows, kv_width), bf16),
            pltpu.VMEM((seq_n, rows, dp_n * depth), bf16),
            pltpu.VMEM((seq_n, rows, kv_width), bf16),
            pltpu.VMEM((dp_n, depth, kv_width), link),
            pltpu.VMEM((dp_n, depth, kv_width), link),
            dma((SPAN + 1,)), dma((SPAN + 1,)), dma((na,)), dma((na,)), dma((na,)), dma((na,)),
            dma((dp_n,)), dma((dp_n,)),
        ],
        compiler_params=pltpu.CompilerParams(
            collective_id=1, has_side_effects=True, vmem_limit_bytes=VMEM_BYTES
        ),
    )(grads, cos_pos, sin_pos, cols_all, target_all)
    return attn_out, loss[0], weight_grad


def solution(mesh):
    both = P(("dp", "seq"), None)
    flat = P(("dp", "seq"))
    return jax.shard_map(
        local,
        mesh=mesh,
        in_specs=(both, both, both, flat, both, P("dp", None), both, both),
        out_specs=(both, flat, both),
        check_vma=False,
    )
```

```python
import functools

import jax
import jax.numpy as jnp
from jax import lax
from jax.experimental import pallas as pl
from jax.experimental.pallas import tpu as pltpu
from jax.sharding import PartitionSpec as P

HEAD_DIM = 128
SPAN = 2
MESH = pl.DeviceIdType.MESH
VMEM_BYTES = 50 * 1024 * 1024

negative = -1e30
rope_base = 500000.0


def angles(positions):
    halfway = HEAD_DIM // 2
    frequency = rope_base ** (-2.0 * jnp.arange(halfway, dtype=jnp.float32) / HEAD_DIM)
    angle = positions.astype(jnp.float32)[:, None] * frequency[None, :]
    cosine = jnp.cos(angle)
    sine = jnp.sin(angle)
    return (
        jnp.concatenate([cosine, cosine], axis=1),
        jnp.concatenate([-sine, sine], axis=1),
    )


def turned(block, cosine, sine):
    return block * cosine + pltpu.roll(block, HEAD_DIM // 2, 1) * sine


def dot(a, b, ca=1, cb=0):
    return lax.dot_general(a, b, (((ca,), (cb,)), ((), ())), preferred_element_type=jnp.float32)


def greet(seq_n, dp_n):
    s = lax.axis_index("seq")
    p = lax.axis_index("dp")
    barrier = pltpu.get_barrier_semaphore()
    for k in range(1, seq_n):
        pl.semaphore_signal(
            barrier, inc=1, device_id=(p, lax.rem(s + k, seq_n)), device_id_type=MESH
        )
    for k in range(1, dp_n):
        pl.semaphore_signal(
            barrier, inc=1, device_id=(lax.rem(p + k, dp_n), s), device_id_type=MESH
        )
    pl.semaphore_wait(barrier, seq_n - 1 + dp_n - 1)


def remote(src, dst, send, recv, p, s):
    return pltpu.make_async_remote_copy(
        src_ref=src, dst_ref=dst, send_sem=send, recv_sem=recv, device_id=(p, s),
        device_id_type=MESH,
    )


def mirror(a, size):
    return (a // size) * size * 2 + size - 1 - a


def mirror_prefix(a, levels, stop):
    held = [a]
    for size in levels:
        if size == stop:
            return held
        held = held + mirror_prefix(mirror(a, size), levels, size)
    return held


def spread(levels, a, peer, send, recv, place, on_hold):
    copies = []
    on_hold(a, 0)
    count = 1
    for size in levels:
        partner = mirror(a, size)
        mine = mirror_prefix(a, levels, size)
        theirs = mirror_prefix(partner, levels, size)
        fresh = []
        for i, shard in enumerate(mine):
            cp = remote(
                place(shard), place(shard), send.at[count + i], recv.at[count + i], *peer(partner)
            )
            cp.start()
            fresh.append(cp)
        for i, shard in enumerate(theirs):
            fresh[i].wait_recv()
            on_hold(shard, count + i)
        copies += fresh
        count += len(mine)
    return copies


def whole_kernel(
    seq_n, dp_n, inside, scale,
    w_ref, hidden_ref, query_ref, value_ref, left_ref, right_ref, cos_ref, sin_ref,
    cols_ref, target_ref, pick_ref, prob_ref, start_ref, cospos_ref, sinpos_ref,
    att_ref, loss_ref, out_ref,
    wall, parcel, got, kparcel, kgot, marks_ref, q_seq, kv_win, cols_all, target_all,
    own, sent, back, sorted_cols, kg, share, arrived,
    wz_s, wz_r, wx_s, wx_r, wy_s, wy_r, wc_s, wc_r,
    par_s, par_r, col_s, col_r, tgt_s, tgt_r, k_s, k_r, sh_s, sh_r,
    b_s, b_r, z_s, z_r, x_s, x_r, d_s, d_r,
):
    s = lax.axis_index("seq")
    p = lax.axis_index("dp")
    rows = query_ref.shape[0]
    qhalf = query_ref.shape[1] // 2
    vhalf = value_ref.shape[1] // 2
    kvn = value_ref.shape[1] // HEAD_DIM
    heads = query_ref.shape[1] // HEAD_DIM
    group = heads // kvn
    slots = got.shape[1]
    cap = slots // 2
    a, b = s // 2, lax.rem(s, 2)
    yb, cc = p // 2, lax.rem(p, 2)
    na, nb = seq_n // 2, dp_n // 2
    levels = []
    while (na >> len(levels)) > 1:
        levels.append(na >> len(levels))
    if inside:
        wall[p, s] = w_ref[...]
    greet(seq_n, dp_n)
    sends = []

    def others():
        return [(k, lax.rem(s + k, seq_n)) for k in range(1, seq_n)]

    tgts = []
    for k, to in others():
        cp = remote(target_ref, target_all.at[s], tgt_s.at[k], tgt_r.at[k], p, to)
        cp.start()
        tgts.append(cp)
    target_all[s] = target_ref[...]

    left = left_ref[...]
    right = right_ref[...]

    def send_queries():
        parcel[...] = (
            (dot(left, query_ref[:, 0:qhalf]) + dot(right, query_ref[:, qhalf:]))
            .astype(jnp.bfloat16).reshape(seq_n, slots, qhalf)
        )
        started = []
        for k, to in others():
            cp = remote(parcel.at[to], got.at[s], par_s.at[k], par_r.at[k], p, to)
            cp.start()
            started.append(cp)
        got[s] = parcel[s]
        kparcel[:, :, vhalf:] = (
            (dot(left, value_ref[:, 0:vhalf]) + dot(right, value_ref[:, vhalf:]))
            .astype(jnp.bfloat16).reshape(seq_n, slots, vhalf)
        )
        return started

    par = []
    if inside:
        cores, ys, xs = [], [], []

        def to_core(y, sh, slot):
            where = wall.at[y * 2 + cc, sh]
            cp = remote(where, where, wc_s.at[slot], wc_r.at[slot], yb * 2 + 1 - cc, s)
            cp.start()
            cores.append(cp)

        def to_y(sh, slot):
            for m in range(1, nb):
                where = wall.at[p, sh]
                cp = remote(
                    where, where, wy_s.at[m, slot], wy_r.at[m, slot],
                    lax.rem(yb + m, nb) * 2 + cc, s,
                )
                cp.start()
                ys.append((cp, m, slot, sh))
            to_core(yb, sh, slot)

        def held_w(shard, index):
            sh = shard * 2 + b
            cp = remote(
                wall.at[p, sh], wall.at[p, sh], wx_s.at[index], wx_r.at[index], p, a * 2 + 1 - b
            )
            cp.start()
            xs.append((cp, index, shard * 2 + 1 - b))
            to_y(sh, 2 * index)

        zc = spread(
            levels, a, lambda t: (p, t * 2 + b), wz_s, wz_r,
            lambda shard: wall.at[p, shard * 2 + b], held_w,
        )
        par = send_queries()
        for cp, index, sh in xs:
            cp.wait_recv()
            to_y(sh, 2 * index + 1)
        for cp, m, slot, sh in list(ys):
            cp.wait_recv()
            to_core(lax.rem(yb - m + nb, nb), sh, m * seq_n + slot)
        for cp in cores:
            cp.wait_recv()
        sends += zc + [c[0] for c in xs] + [c[0] for c in ys] + cores
        weights = wall[...].reshape(hidden_ref.shape[1], -1)
    else:
        par = send_queries()
        weights = w_ref[...]

    projected = dot(hidden_ref[...], weights)
    cosine = cos_ref[...]
    sine = sin_ref[...]
    keys = jnp.concatenate(
        [
            turned(projected[:, g * HEAD_DIM:(g + 1) * HEAD_DIM], cosine, sine)
            for g in range(kvn)
        ],
        axis=1,
    ).astype(jnp.bfloat16)
    kparcel[:, :, 0:vhalf] = (
        (dot(left, keys[:, 0:vhalf]) + dot(right, keys[:, vhalf:]))
        .astype(jnp.bfloat16).reshape(seq_n, slots, vhalf)
    )
    ks = []
    for k, to in others():
        cp = remote(kparcel.at[to], kgot.at[s], k_s.at[k], k_r.at[k], p, to)
        cp.start()
        ks.append(cp)
    kgot[s] = kparcel[s]

    for cp in tgts:
        cp.wait_recv()
    square = (rows, rows)
    down = lax.broadcasted_iota(jnp.int32, square, 0)
    across = lax.broadcasted_iota(jnp.int32, square, 1)
    before = jnp.where(down < across, 1.0, 0.0).astype(jnp.bfloat16)
    slot_id = lax.broadcasted_iota(jnp.int32, (slots, rows), 0)
    slot_id = jnp.where(slot_id >= cap, slot_id - cap, slot_id).astype(jnp.float32)
    for j in range(seq_n):
        offset = target_all[j] - s * rows
        mine = (offset >= 0) & (offset < rows)
        flag = jnp.where(mine, 1.0, 0.0)
        rank = dot(flag.astype(jnp.bfloat16), before)
        rank = jnp.where(mine, rank, -1.0)
        filled = jnp.where(slot_id == rank[0:1, :], 1.0, 0.0).astype(jnp.bfloat16)
        at = jnp.where(down == offset[0:1, :], 1.0, 0.0).astype(jnp.bfloat16)
        marks_ref[j] = dot(filled, at, 1, 1).astype(jnp.bfloat16)
    marks = marks_ref[...].reshape(seq_n * slots, rows)
    place = lax.rem(lax.broadcasted_iota(jnp.int32, marks.shape, 0), slots)
    first = jnp.where(place < cap, marks, jnp.zeros_like(marks))
    second = jnp.where(place < cap, jnp.zeros_like(marks), marks)

    for cp in par:
        cp.wait_recv()
    for half, mark in ((0, first), (1, second)):
        base = half * (heads // 2)
        settled = dot(mark, got[...].reshape(seq_n * slots, qhalf), 0, 0).astype(jnp.bfloat16)
        for h in range(heads // 2):
            head = base + h
            q_seq[head // group, (head % group) * rows:(head % group + 1) * rows, :] = settled[
                :, h * HEAD_DIM:(h + 1) * HEAD_DIM
            ]
    for cp in ks:
        cp.wait_recv()
    for half, mark in ((0, first), (1, second)):
        settled = dot(mark, kgot[...].reshape(seq_n * slots, 2 * vhalf), 0, 0).astype(jnp.bfloat16)
        for h in range(kvn):
            head = (h // (kvn // 2)) * kvn + half * (kvn // 2) + h % (kvn // 2)
            kv_win[head, SPAN * rows:, :] = settled[:, h * HEAD_DIM:(h + 1) * HEAD_DIM]

    def shift(by):
        return remote(
            kv_win.at[:, SPAN * rows:(SPAN + 1) * rows, :],
            kv_win.at[:, (SPAN - by) * rows:(SPAN - by + 1) * rows, :],
            sh_s.at[by], sh_r.at[by], p, lax.rem(s + by, seq_n),
        )

    for by in range(1, SPAN + 1):
        @pl.when(s + by < seq_n)
        def _(by=by):
            shift(by).start()

        @pl.when(s < by)
        def _(by=by):
            kv_win[:, (SPAN - by) * rows:(SPAN - by + 1) * rows, :] = jnp.zeros(
                (2 * kvn, rows, HEAD_DIM), jnp.bfloat16
            )

        @pl.when(s + by >= seq_n)
        def _(by=by):
            back[by - 1] = jnp.zeros(back.shape[1:], jnp.bfloat16)
    cols = []
    for k, to in others():
        cp = remote(cols_ref.at[to], cols_all.at[s], col_s.at[k], col_r.at[k], p, to)
        cp.start()
        cols.append(cp)
    cols_all[s] = cols_ref[s]
    for by in range(1, SPAN + 1):
        @pl.when(s >= by)
        def _(by=by):
            shift(by).wait_recv()

    width = (SPAN + 1) * rows
    lanes = group * rows
    scaling = HEAD_DIM ** (-0.5)
    loss_ref[...] = jnp.zeros(loss_ref.shape, jnp.float32)

    def give(by, g):
        return remote(
            sent.at[by - 1, g], back.at[by - 1, g], b_s.at[by - 1, g], b_r.at[by - 1, g], p,
            lax.rem(s - by + seq_n, seq_n),
        )

    def attend(g, carry):
        queries = q_seq[g]
        score = dot(kv_win[g], queries, 1, 1) * scaling
        spot = lax.broadcasted_iota(jnp.int32, (width, lanes), 0)
        last = lax.rem(lax.broadcasted_iota(jnp.int32, (1, lanes), 1), rows) + (width - rows)
        allowed = (spot >= start_ref[...]) & (spot <= last)
        held = jnp.where(allowed, score, negative)
        top = jnp.max(held, axis=0, keepdims=True)
        raised = jnp.exp(held - top)
        total = jnp.sum(raised, axis=0, keepdims=True)
        lse = top + jnp.log(total)
        weight = raised * (1.0 / total)
        prob = prob_ref[g]
        pick = pick_ref[g]
        table = jnp.zeros((width, lanes), jnp.float32)
        for k in range(prob.shape[0]):
            table += jnp.where(spot == pick[k:k + 1, :], prob[k:k + 1, :], 0.0)
        mass = jnp.sum(prob, axis=0, keepdims=True)
        entropy = jnp.sum(prob * jnp.log(prob), axis=0, keepdims=True)
        picked = jnp.sum(table * score, axis=0, keepdims=True)
        loss = (entropy - picked + mass * lse) * (1.0 / heads)
        part = loss[:, 0:rows]
        for h in range(1, group):
            part += loss[:, h * rows:(h + 1) * rows]
        loss_ref[...] += part
        slope = ((weight * mass - table) * (1.0 / heads)).astype(jnp.bfloat16)
        grad = dot(slope, queries) * scaling
        own[g] = grad[SPAN * rows:, :]
        for by in range(1, SPAN + 1):
            sent[by - 1, g] = grad[(SPAN - by) * rows:(SPAN - by + 1) * rows, :].astype(
                jnp.bfloat16
            )

            @pl.when(s >= by)
            def _(by=by):
                give(by, g).start()

        output = dot(weight.astype(jnp.bfloat16), kv_win[kvn + g], 0, 0).astype(jnp.bfloat16)
        for h in range(group):
            lane = pl.multiple_of((g * group + h) * HEAD_DIM, HEAD_DIM)
            att_ref[:, pl.ds(lane, HEAD_DIM)] = output[h * rows:(h + 1) * rows, :]
        return carry

    lax.fori_loop(0, kvn, attend, 0)

    for cp in cols:
        cp.wait_recv()
    count = seq_n * rows
    total = jnp.zeros((count, cols_ref.shape[2]), jnp.float32)
    spot = lax.broadcasted_iota(jnp.int32, (count, rows), 0)
    for j in range(seq_n):
        hit = jnp.where(spot == target_all[j, 0:1, :], 1.0, 0.0).astype(jnp.bfloat16)
        total += dot(hit, cols_all[j])
    sorted_cols[...] = total.astype(jnp.bfloat16).reshape(sorted_cols.shape)

    for by in range(1, SPAN + 1):
        @pl.when(s + by < seq_n)
        def _(by=by):
            for g in range(kvn):
                give(by, g).wait_recv()
    cosine = cospos_ref[...]
    sine = -sinpos_ref[...]
    for g in range(kvn):
        rotated = own[g]
        for by in range(1, SPAN + 1):
            rotated += back[by - 1, g].astype(jnp.float32)
        kg[s, :, g * HEAD_DIM:(g + 1) * HEAD_DIM] = turned(rotated, cosine, sine).astype(
            jnp.bfloat16
        )
    pairs = []
    terms = []

    def held_kg(shard, index):
        sh = shard * 2 + b
        cp = remote(kg.at[sh], kg.at[sh], x_s.at[index], x_r.at[index], p, a * 2 + 1 - b)
        cp.start()
        pairs.append((cp, shard * 2 + 1 - b))
        terms.append(sh)

    zk = spread(
        levels, a, lambda t: (p, t * 2 + b), z_s, z_r, lambda shard: kg.at[shard * 2 + b], held_kg
    )
    result = None
    for sh in terms:
        term = dot(sorted_cols[sh], kg[sh], 0, 0)
        result = term if result is None else result + term
    for cp, sh in pairs:
        cp.wait_recv()
        result += dot(sorted_cols[sh], kg[sh], 0, 0)
    result *= scale
    depth = share.shape[1]
    for m in range(dp_n):
        share[m] = result[m * depth:(m + 1) * depth, :].astype(share.dtype)
    ds = []
    for m in range(1, dp_n):
        to = lax.rem(p + m, dp_n)
        cp = remote(share.at[to], arrived.at[m], d_s.at[m], d_r.at[m], to, s)
        cp.start()
        ds.append(cp)
    final = share[p].astype(jnp.float32)
    for m in range(1, dp_n):
        ds[m - 1].wait_recv()
        final += arrived[m].astype(jnp.float32)
    out_ref[...] = final
    for cp in sends + tgts + par + ks + cols + zk + [c[0] for c in pairs] + ds:
        cp.wait_send()
    for by in range(1, SPAN + 1):
        @pl.when(s + by < seq_n)
        def _(by=by):
            shift(by).wait_send()

        @pl.when(s >= by)
        def _(by=by):
            for g in range(kvn):
                give(by, g).wait_send()


def local(
    hidden, queries, values, row_target, key_weight, dialogue_lengths, teacher_pick, teacher_prob
):
    rows = hidden.shape[0]
    seq_n = lax.axis_size("seq")
    dp_n = lax.axis_size("dp")
    s = lax.axis_index("seq")
    depth, kv_width = key_weight.shape
    capacity = rows // seq_n + rows // (2 * seq_n)
    capacity = -(-capacity // 8) * 8
    heads = queries.shape[1] // HEAD_DIM
    kvn = kv_width // HEAD_DIM
    group = heads // kvn
    top = teacher_pick.shape[1] // heads
    slots = 2 * capacity
    vmem = pl.BlockSpec(memory_space=pltpu.VMEM)
    dma = pltpu.SemaphoreType.DMA
    bf16 = jnp.bfloat16

    destination = row_target // rows
    order = jnp.arange(rows, dtype=jnp.int32)
    earlier = (destination[None, :] == destination[:, None]) & (order[None, :] < order[:, None])
    rank = jnp.sum(earlier.astype(jnp.int32), axis=1)
    slot = destination * slots + rank
    every = jnp.arange(seq_n * slots, dtype=jnp.int32)[:, None]
    left = (every == slot[None, :]).astype(bf16)
    right = (every == slot[None, :] + capacity).astype(bf16)
    cos_row, sin_row = angles(row_target)
    columns = hidden.reshape(rows, dp_n, seq_n, depth).transpose(2, 0, 1, 3)
    columns = columns.reshape(seq_n, rows, dp_n * depth)
    target_tile = jnp.broadcast_to(row_target[None, :], (8, rows))

    positions = s * rows + order
    ending = jnp.cumsum(dialogue_lengths[0])
    starts = jnp.sum(
        jnp.where(ending[None, :] <= positions[:, None], dialogue_lengths[0][None, :], 0), axis=1
    )
    base = (s - SPAN) * rows
    reach = (positions - starts + 1)[:, None]
    picks = (starts[:, None] - base + teacher_pick % reach).reshape(rows, kvn, group, top)
    picks = picks.transpose(1, 3, 2, 0).reshape(kvn, top, group * rows)
    probs = teacher_prob.reshape(rows, kvn, group, top).transpose(1, 3, 2, 0)
    probs = probs.reshape(kvn, top, group * rows)
    lower = jnp.tile(starts - base, group)[None, :]
    cos_pos, sin_pos = angles(positions)

    inside = depth % 16 == 0
    weight_in = key_weight
    if not inside:
        weight_in = lax.all_gather(key_weight, ("dp", "seq"), axis=0, tiled=True)
    qhalf = queries.shape[1] // 2
    na, nb = seq_n // 2, dp_n // 2
    wall = (dp_n, seq_n, depth, kv_width) if inside else (8, 128)
    link = bf16 if inside else jnp.float32
    semaphores = (
        [(na,)] * 4 + [(nb, seq_n)] * 2 + [(nb * seq_n,)] * 2 + [(seq_n,)] * 8 + [(SPAN + 1,)] * 2
        + [(SPAN, kvn)] * 2 + [(na,)] * 4 + [(dp_n,)] * 2
    )
    attn_out, loss, weight_grad = pl.pallas_call(
        functools.partial(
            whole_kernel, seq_n, dp_n, inside, (rows * seq_n * dp_n) ** (-0.5)
        ),
        out_shape=(
            jax.ShapeDtypeStruct((rows, heads * HEAD_DIM), bf16),
            jax.ShapeDtypeStruct((1, rows), jnp.float32),
            jax.ShapeDtypeStruct((depth, kv_width), jnp.float32),
        ),
        in_specs=[vmem] * 15,
        out_specs=(vmem,) * 3,
        scratch_shapes=[
            pltpu.VMEM(wall, bf16),
            pltpu.VMEM((seq_n, slots, qhalf), bf16),
            pltpu.VMEM((seq_n, slots, qhalf), bf16),
            pltpu.VMEM((seq_n, slots, kv_width), bf16),
            pltpu.VMEM((seq_n, slots, kv_width), bf16),
            pltpu.VMEM((seq_n, slots, rows), bf16),
            pltpu.VMEM((kvn, group * rows, HEAD_DIM), bf16),
            pltpu.VMEM((2 * kvn, (SPAN + 1) * rows, HEAD_DIM), bf16),
            pltpu.VMEM(columns.shape, bf16),
            pltpu.VMEM((seq_n, 8, rows), jnp.int32),
            pltpu.VMEM((kvn, rows, HEAD_DIM), jnp.float32),
            pltpu.VMEM((SPAN, kvn, rows, HEAD_DIM), bf16),
            pltpu.VMEM((SPAN, kvn, rows, HEAD_DIM), bf16),
            pltpu.VMEM((seq_n, rows, dp_n * depth), bf16),
            pltpu.VMEM((seq_n, rows, kv_width), bf16),
            pltpu.VMEM((dp_n, depth, kv_width), link),
            pltpu.VMEM((dp_n, depth, kv_width), link),
        ] + [dma(shape) for shape in semaphores],
        compiler_params=pltpu.CompilerParams(
            collective_id=0, has_side_effects=True, vmem_limit_bytes=VMEM_BYTES
        ),
    )(
        weight_in, hidden, queries, values, left, right, cos_row, sin_row, columns, target_tile,
        picks, probs, lower, cos_pos, sin_pos,
    )
    return attn_out, loss[0], weight_grad


def solution(mesh):
    both = P(("dp", "seq"), None)
    flat = P(("dp", "seq"))
    return jax.shard_map(
        local,
        mesh=mesh,
        in_specs=(both, both, both, flat, both, P("dp", None), both, both),
        out_specs=(both, flat, both),
        check_vma=False,
    )
```

```python
import functools

import jax
import jax.numpy as jnp
from jax import lax
from jax.experimental import pallas as pl
from jax.experimental.pallas import tpu as pltpu
from jax.sharding import PartitionSpec as P

HEAD_DIM = 128
SPAN = 2
MESH = pl.DeviceIdType.MESH
VMEM_BYTES = 50 * 1024 * 1024

negative = -1e30
rope_base = 500000.0


def angles(positions):
    halfway = HEAD_DIM // 2
    frequency = rope_base ** (-2.0 * jnp.arange(halfway, dtype=jnp.float32) / HEAD_DIM)
    angle = positions.astype(jnp.float32)[:, None] * frequency[None, :]
    cosine = jnp.cos(angle)
    sine = jnp.sin(angle)
    return (
        jnp.concatenate([cosine, cosine], axis=1),
        jnp.concatenate([-sine, sine], axis=1),
    )


def turned(block, cosine, sine):
    return block * cosine + pltpu.roll(block, HEAD_DIM // 2, 1) * sine


def dot(a, b, ca=1, cb=0):
    return lax.dot_general(a, b, (((ca,), (cb,)), ((), ())), preferred_element_type=jnp.float32)


def greet(seq_n, dp_n):
    s = lax.axis_index("seq")
    p = lax.axis_index("dp")
    barrier = pltpu.get_barrier_semaphore()
    for k in range(1, seq_n):
        pl.semaphore_signal(
            barrier, inc=1, device_id=(p, lax.rem(s + k, seq_n)), device_id_type=MESH
        )
    for k in range(1, dp_n):
        pl.semaphore_signal(
            barrier, inc=1, device_id=(lax.rem(p + k, dp_n), s), device_id_type=MESH
        )
    return barrier


def remote(src, dst, send, recv, p, s):
    return pltpu.make_async_remote_copy(
        src_ref=src, dst_ref=dst, send_sem=send, recv_sem=recv, device_id=(p, s),
        device_id_type=MESH,
    )


def mirror(a, size):
    return (a // size) * size * 2 + size - 1 - a


def mirror_prefix(a, levels, stop):
    held = [a]
    for size in levels:
        if size == stop:
            return held
        held = held + mirror_prefix(mirror(a, size), levels, size)
    return held


def spread(levels, a, peer, send, recv, place, on_hold):
    copies = []
    on_hold(a, 0)
    count = 1
    for size in levels:
        partner = mirror(a, size)
        mine = mirror_prefix(a, levels, size)
        theirs = mirror_prefix(partner, levels, size)
        fresh = []
        for i, shard in enumerate(mine):
            cp = remote(
                place(shard), place(shard), send.at[count + i], recv.at[count + i], *peer(partner)
            )
            cp.start()
            fresh.append(cp)
        for i, shard in enumerate(theirs):
            fresh[i].wait_recv()
            on_hold(shard, count + i)
        copies += fresh
        count += len(mine)
    return copies


def whole_kernel(
    seq_n, dp_n, inside, scale,
    w_ref, hidden_ref, query_ref, value_ref, row_ref, cos_ref, sin_ref,
    cols_ref, drawn_ref, given_ref, lower_ref, cospos_ref, sinpos_ref,
    att_ref, loss_ref, out_ref,
    wall, parcel, got, vparcel, vgot, kparcel, kgot, target_ref, pick_ref, prob_ref, marks_ref, q_seq, kv_win, cols_all, target_all,
    own, sent, back, sorted_cols, kg, share, arrived,
    wz_s, wz_r, wx_s, wx_r, wy_s, wy_r, wc_s, wc_r,
    par_s, par_r, v_s, v_r, col_s, col_r, tgt_s, tgt_r, k_s, k_r, sh_s, sh_r,
    b_s, b_r, z_s, z_r, x_s, x_r, d_s, d_r,
):
    s = lax.axis_index("seq")
    p = lax.axis_index("dp")
    rows = query_ref.shape[0]
    qhalf = query_ref.shape[1] // 2
    vhalf = value_ref.shape[1] // 2
    kvn = value_ref.shape[1] // HEAD_DIM
    heads = query_ref.shape[1] // HEAD_DIM
    group = heads // kvn
    slots = got.shape[1]
    cap = slots // 2
    a, b = s // 2, lax.rem(s, 2)
    yb, cc = p // 2, lax.rem(p, 2)
    na, nb = seq_n // 2, dp_n // 2
    levels = []
    while (na >> len(levels)) > 1:
        levels.append(na >> len(levels))
    barrier = greet(seq_n, dp_n)
    if inside:
        wall[p, s] = w_ref[...]
    target_ref[...] = jnp.broadcast_to(row_ref[...], target_ref.shape)
    sends = []

    def others():
        return [(k, lax.rem(s + k, seq_n)) for k in range(1, seq_n)]

    tgts = []
    target_all[s] = target_ref[...]

    square = (rows, rows)
    down = lax.broadcasted_iota(jnp.int32, square, 0)
    across = lax.broadcasted_iota(jnp.int32, square, 1)
    before = jnp.where(down < across, 1.0, 0.0).astype(jnp.bfloat16)

    def packers():
        target = row_ref[...]
        block = lax.broadcasted_iota(jnp.int32, (seq_n, rows), 0) * rows
        here = jnp.where((target >= block) & (target < block + rows), 1.0, 0.0)
        seen = dot(here.astype(jnp.bfloat16), before)
        index = lax.broadcasted_iota(jnp.int32, (seq_n, rows), 0).astype(jnp.float32)
        slot = jnp.sum(here * (seen + index * slots), axis=0, keepdims=True)
        every = lax.broadcasted_iota(jnp.int32, (seq_n * slots, rows), 0).astype(jnp.float32)
        return (
            jnp.where(every == slot, 1.0, 0.0).astype(jnp.bfloat16),
            jnp.where(every == slot + cap, 1.0, 0.0).astype(jnp.bfloat16),
        )

    lower = lower_ref[...]
    top_n = drawn_ref.shape[1] // heads

    def labels():
        lane = lax.broadcasted_iota(jnp.int32, (1, rows), 1)
        reach = (lane + SPAN * rows - lower + 1).astype(jnp.float32)
        drawn = jnp.transpose(drawn_ref[...].astype(jnp.float32))
        left_over = drawn - jnp.floor(drawn * (1.0 / reach)) * reach
        left_over = jnp.where(left_over < 0.0, left_over + reach, left_over)
        left_over = jnp.where(left_over >= reach, left_over - reach, left_over)
        chosen = left_over.astype(jnp.int32) + lower
        given = jnp.transpose(given_ref[...])
        for h in range(heads):
            place = slice((h % group) * rows, (h % group + 1) * rows)
            pick_ref[h // group, :, place] = chosen[h * top_n:(h + 1) * top_n, :]
            prob_ref[h // group, :, place] = given[h * top_n:(h + 1) * top_n, :]

    def places():
        for cp in tgts:
            cp.wait_recv()
        slot_id = lax.broadcasted_iota(jnp.int32, (slots, rows), 0)
        slot_id = jnp.where(slot_id >= cap, slot_id - cap, slot_id).astype(jnp.float32)
        for j in range(seq_n):
            offset = target_all[j] - s * rows
            mine = (offset >= 0) & (offset < rows)
            flag = jnp.where(mine, 1.0, 0.0)
            rank = dot(flag.astype(jnp.bfloat16), before)
            rank = jnp.where(mine, rank, -1.0)
            filled = jnp.where(slot_id == rank[0:1, :], 1.0, 0.0).astype(jnp.bfloat16)
            at = jnp.where(down == offset[0:1, :], 1.0, 0.0).astype(jnp.bfloat16)
            marks_ref[j] = dot(filled, at, 1, 1).astype(jnp.bfloat16)

    def send_rows():
        started = ([], [])
        for k, to in others():
            cp = remote(vparcel.at[to], vgot.at[s], v_s.at[k], v_r.at[k], p, to)
            cp.start()
            started[0].append(cp)
        for k, to in others():
            cp = remote(parcel.at[to], got.at[s], par_s.at[k], par_r.at[k], p, to)
            cp.start()
            started[1].append(cp)
        return started

    left, right = packers()
    vparcel[...] = (
        (dot(left, value_ref[:, 0:vhalf]) + dot(right, value_ref[:, vhalf:]))
        .astype(jnp.bfloat16).reshape(seq_n, slots, vhalf)
    )
    vgot[s] = vparcel[s]
    parcel[...] = (
        (dot(left, query_ref[:, 0:qhalf]) + dot(right, query_ref[:, qhalf:]))
        .astype(jnp.bfloat16).reshape(seq_n, slots, qhalf)
    )
    got[s] = parcel[s]
    pl.semaphore_wait(barrier, seq_n - 1 + dp_n - 1)
    for k, to in others():
        cp = remote(target_ref, target_all.at[s], tgt_s.at[k], tgt_r.at[k], p, to)
        cp.start()
        tgts.append(cp)

    if inside:
        cores, ys, xs = [], [], []

        def to_core(y, sh, slot):
            where = wall.at[y * 2 + cc, sh]
            cp = remote(where, where, wc_s.at[slot], wc_r.at[slot], yb * 2 + 1 - cc, s)
            cp.start()
            cores.append(cp)

        def to_y(sh, slot):
            for m in range(1, nb):
                where = wall.at[p, sh]
                cp = remote(
                    where, where, wy_s.at[m, slot], wy_r.at[m, slot],
                    lax.rem(yb + m, nb) * 2 + cc, s,
                )
                cp.start()
                ys.append((cp, m, slot, sh))
            to_core(yb, sh, slot)

        def held_w(shard, index):
            sh = shard * 2 + b
            cp = remote(
                wall.at[p, sh], wall.at[p, sh], wx_s.at[index], wx_r.at[index], p, a * 2 + 1 - b
            )
            cp.start()
            xs.append((cp, index, shard * 2 + 1 - b))
            to_y(sh, 2 * index)

        zc = spread(
            levels, a, lambda t: (p, t * 2 + b), wz_s, wz_r,
            lambda shard: wall.at[p, shard * 2 + b], held_w,
        )
        vs, par = send_rows()
        for cp, index, sh in xs:
            cp.wait_recv()
            to_y(sh, 2 * index + 1)
        for cp, m, slot, sh in list(ys):
            cp.wait_recv()
            to_core(lax.rem(yb - m + nb, nb), sh, m * seq_n + slot)
        places()
        labels()
        for cp in cores:
            cp.wait_recv()
        sends += zc + [c[0] for c in xs] + [c[0] for c in ys] + cores
        weights = wall[...].reshape(hidden_ref.shape[1], -1)
    else:
        vs, par = send_rows()
        places()
        labels()
        weights = w_ref[...]

    projected = dot(hidden_ref[...], weights)
    cosine = cos_ref[...]
    sine = sin_ref[...]
    keys = jnp.concatenate(
        [
            turned(projected[:, g * HEAD_DIM:(g + 1) * HEAD_DIM], cosine, sine)
            for g in range(kvn)
        ],
        axis=1,
    ).astype(jnp.bfloat16)
    kparcel[...] = (
        (dot(left, keys[:, 0:vhalf]) + dot(right, keys[:, vhalf:]))
        .astype(jnp.bfloat16).reshape(seq_n, slots, vhalf)
    )
    ks = []
    for k, to in others():
        cp = remote(kparcel.at[to], kgot.at[s], k_s.at[k], k_r.at[k], p, to)
        cp.start()
        ks.append(cp)
    kgot[s] = kparcel[s]

    marks = marks_ref[...].reshape(seq_n * slots, rows)
    place = lax.rem(lax.broadcasted_iota(jnp.int32, marks.shape, 0), slots)
    first = jnp.where(place < cap, marks, jnp.zeros_like(marks))
    second = jnp.where(place < cap, jnp.zeros_like(marks), marks)

    held_rows = seq_n * slots

    def settle(ref, first_head):
        block = ref[...].reshape(held_rows, vhalf)
        for half, mark in ((0, first), (1, second)):
            settled = dot(mark, block, 0, 0).astype(jnp.bfloat16)
            for h in range(kvn // 2):
                kv_win[first_head + half * (kvn // 2) + h, SPAN * rows:, :] = settled[
                    :, h * HEAD_DIM:(h + 1) * HEAD_DIM
                ]

    def shift(by, head):
        return remote(
            kv_win.at[head, SPAN * rows:(SPAN + 1) * rows, :],
            kv_win.at[head, (SPAN - by) * rows:(SPAN - by + 1) * rows, :],
            sh_s.at[by - 1, head], sh_r.at[by - 1, head], p, lax.rem(s + by, seq_n),
        )

    def shift_all(first_head):
        for head in range(kvn):
            for by in range(1, SPAN + 1):
                @pl.when(s + by < seq_n)
                def _(by=by, head=head):
                    shift(by, first_head + head).start()

    for cp in vs:
        cp.wait_recv()
    settle(vgot, kvn)
    shift_all(kvn)
    for by in range(1, SPAN + 1):
        @pl.when(s < by)
        def _(by=by):
            kv_win[:, (SPAN - by) * rows:(SPAN - by + 1) * rows, :] = jnp.zeros(
                (2 * kvn, rows, HEAD_DIM), jnp.bfloat16
            )

        @pl.when(s + by >= seq_n)
        def _(by=by):
            back[by - 1] = jnp.zeros(back.shape[1:], jnp.bfloat16)
    for cp in ks:
        cp.wait_recv()
    settle(kgot, 0)
    shift_all(0)
    for cp in par:
        cp.wait_recv()
    for half, mark in ((0, first), (1, second)):
        base = half * (heads // 2)
        settled = dot(mark, got[...].reshape(held_rows, qhalf), 0, 0).astype(jnp.bfloat16)
        for h in range(heads // 2):
            head = base + h
            q_seq[head // group, (head % group) * rows:(head % group + 1) * rows, :] = settled[
                :, h * HEAD_DIM:(h + 1) * HEAD_DIM
            ]
    cols = []
    for k, to in others():
        cp = remote(cols_ref.at[to], cols_all.at[s], col_s.at[k], col_r.at[k], p, to)
        cp.start()
        cols.append(cp)
    cols_all[s] = cols_ref[s]
    starting = jnp.concatenate([lower] * group, axis=1)

    width = (SPAN + 1) * rows
    lanes = group * rows
    scaling = HEAD_DIM ** (-0.5)
    loss_ref[...] = jnp.zeros(loss_ref.shape, jnp.float32)

    def give(by, g):
        return remote(
            sent.at[by - 1, g], back.at[by - 1, g], b_s.at[by - 1, g], b_r.at[by - 1, g], p,
            lax.rem(s - by + seq_n, seq_n),
        )

    def attend(g, carry):
        for by in range(1, SPAN + 1):
            @pl.when(s >= by)
            def _(by=by):
                shift(by, g).wait_recv()
                shift(by, kvn + g).wait_recv()

        queries = q_seq[g]
        score = dot(kv_win[g], queries, 1, 1) * scaling
        spot = lax.broadcasted_iota(jnp.int32, (width, lanes), 0)
        last = lax.rem(lax.broadcasted_iota(jnp.int32, (1, lanes), 1), rows) + (width - rows)
        allowed = (spot >= starting) & (spot <= last)
        held = jnp.where(allowed, score, negative)
        top = jnp.max(held, axis=0, keepdims=True)
        raised = jnp.exp(held - top)
        total = jnp.sum(raised, axis=0, keepdims=True)
        lse = top + jnp.log(total)
        weight = raised * (1.0 / total)
        prob = prob_ref[g]
        pick = pick_ref[g]
        table = jnp.zeros((width, lanes), jnp.float32)
        for k in range(prob.shape[0]):
            table += jnp.where(spot == pick[k:k + 1, :], prob[k:k + 1, :], 0.0)
        mass = jnp.sum(prob, axis=0, keepdims=True)
        entropy = jnp.sum(prob * jnp.log(prob), axis=0, keepdims=True)
        picked = jnp.sum(table * score, axis=0, keepdims=True)
        loss = (entropy - picked + mass * lse) * (1.0 / heads)
        part = loss[:, 0:rows]
        for h in range(1, group):
            part += loss[:, h * rows:(h + 1) * rows]
        loss_ref[...] += part
        slope = ((weight * mass - table) * (1.0 / heads)).astype(jnp.bfloat16)
        grad = dot(slope, queries) * scaling
        own[g] = grad[SPAN * rows:, :]
        for by in range(1, SPAN + 1):
            sent[by - 1, g] = grad[(SPAN - by) * rows:(SPAN - by + 1) * rows, :].astype(
                jnp.bfloat16
            )

            @pl.when(s >= by)
            def _(by=by):
                give(by, g).start()

        output = dot(weight.astype(jnp.bfloat16), kv_win[kvn + g], 0, 0).astype(jnp.bfloat16)
        for h in range(group):
            lane = pl.multiple_of((g * group + h) * HEAD_DIM, HEAD_DIM)
            att_ref[:, pl.ds(lane, HEAD_DIM)] = output[h * rows:(h + 1) * rows, :]
        return carry

    lax.fori_loop(0, kvn, attend, 0)

    for by in range(1, SPAN + 1):
        @pl.when(s + by < seq_n)
        def _(by=by):
            for g in range(kvn):
                give(by, g).wait_recv()
    cosine = cospos_ref[...]
    sine = -sinpos_ref[...]
    for g in range(kvn):
        rotated = own[g]
        for by in range(1, SPAN + 1):
            rotated += back[by - 1, g].astype(jnp.float32)
        kg[s, :, g * HEAD_DIM:(g + 1) * HEAD_DIM] = turned(rotated, cosine, sine).astype(
            jnp.bfloat16
        )
    pairs = []
    terms = []

    def held_kg(shard, index):
        sh = shard * 2 + b
        cp = remote(kg.at[sh], kg.at[sh], x_s.at[index], x_r.at[index], p, a * 2 + 1 - b)
        cp.start()
        pairs.append((cp, shard * 2 + 1 - b))
        terms.append(sh)

    zk = spread(
        levels, a, lambda t: (p, t * 2 + b), z_s, z_r, lambda shard: kg.at[shard * 2 + b], held_kg
    )
    for cp in cols:
        cp.wait_recv()
    count = seq_n * rows
    total = jnp.zeros((count, cols_ref.shape[2]), jnp.float32)
    spot = lax.broadcasted_iota(jnp.int32, (count, rows), 0)
    for j in range(seq_n):
        hit = jnp.where(spot == target_all[j, 0:1, :], 1.0, 0.0).astype(jnp.bfloat16)
        total += dot(hit, cols_all[j])
    sorted_cols[...] = total.astype(jnp.bfloat16).reshape(sorted_cols.shape)
    result = None
    for sh in terms:
        term = dot(sorted_cols[sh], kg[sh], 0, 0)
        result = term if result is None else result + term
    for cp, sh in pairs:
        cp.wait_recv()
        result += dot(sorted_cols[sh], kg[sh], 0, 0)
    result *= scale
    depth = share.shape[1]
    for m in range(dp_n):
        share[m] = result[m * depth:(m + 1) * depth, :].astype(share.dtype)
    ds = []
    for m in range(1, dp_n):
        to = lax.rem(p + m, dp_n)
        cp = remote(share.at[to], arrived.at[m], d_s.at[m], d_r.at[m], to, s)
        cp.start()
        ds.append(cp)
    final = share[p].astype(jnp.float32)
    for m in range(1, dp_n):
        ds[m - 1].wait_recv()
        final += arrived[m].astype(jnp.float32)
    out_ref[...] = final
    for cp in sends + tgts + vs + par + ks + cols + zk + [c[0] for c in pairs] + ds:
        cp.wait_send()
    for by in range(1, SPAN + 1):
        @pl.when(s + by < seq_n)
        def _(by=by):
            for head in range(2 * kvn):
                shift(by, head).wait_send()

        @pl.when(s >= by)
        def _(by=by):
            for g in range(kvn):
                give(by, g).wait_send()


def local(
    hidden, queries, values, row_target, key_weight, dialogue_lengths, teacher_pick, teacher_prob
):
    rows = hidden.shape[0]
    seq_n = lax.axis_size("seq")
    dp_n = lax.axis_size("dp")
    s = lax.axis_index("seq")
    depth, kv_width = key_weight.shape
    capacity = rows // seq_n + rows // (2 * seq_n)
    capacity = -(-capacity // 8) * 8
    heads = queries.shape[1] // HEAD_DIM
    kvn = kv_width // HEAD_DIM
    group = heads // kvn
    top = teacher_pick.shape[1] // heads
    slots = 2 * capacity
    vmem = pl.BlockSpec(memory_space=pltpu.VMEM)
    dma = pltpu.SemaphoreType.DMA
    bf16 = jnp.bfloat16

    order = jnp.arange(rows, dtype=jnp.int32)
    cos_row, sin_row = angles(row_target)
    columns = hidden.reshape(rows, dp_n, seq_n, depth).transpose(2, 0, 1, 3)
    columns = columns.reshape(seq_n, rows, dp_n * depth)

    positions = s * rows + order
    ending = jnp.cumsum(dialogue_lengths[0])
    starts = jnp.sum(
        jnp.where(ending[None, :] <= positions[:, None], dialogue_lengths[0][None, :], 0), axis=1
    )
    base = (s - SPAN) * rows
    lower = (starts - base)[None, :]
    cos_pos, sin_pos = angles(positions)

    inside = depth % 16 == 0
    weight_in = key_weight
    if not inside:
        weight_in = lax.all_gather(key_weight, ("dp", "seq"), axis=0, tiled=True)
    qhalf = queries.shape[1] // 2
    na, nb = seq_n // 2, dp_n // 2
    wall = (dp_n, seq_n, depth, kv_width) if inside else (8, 128)
    link = bf16 if inside else jnp.float32
    semaphores = (
        [(na,)] * 4 + [(nb, seq_n)] * 2 + [(nb * seq_n,)] * 2 + [(seq_n,)] * 10
        + [(SPAN, 2 * kvn)] * 2 + [(SPAN, kvn)] * 2 + [(na,)] * 4 + [(dp_n,)] * 2
    )
    attn_out, loss, weight_grad = pl.pallas_call(
        functools.partial(
            whole_kernel, seq_n, dp_n, inside, (rows * seq_n * dp_n) ** (-0.5)
        ),
        out_shape=(
            jax.ShapeDtypeStruct((rows, heads * HEAD_DIM), bf16),
            jax.ShapeDtypeStruct((1, rows), jnp.float32),
            jax.ShapeDtypeStruct((depth, kv_width), jnp.float32),
        ),
        in_specs=[vmem] * 13,
        out_specs=(vmem,) * 3,
        scratch_shapes=[
            pltpu.VMEM(wall, bf16),
            pltpu.VMEM((seq_n, slots, qhalf), bf16),
            pltpu.VMEM((seq_n, slots, qhalf), bf16),
            pltpu.VMEM((seq_n, slots, kv_width // 2), bf16),
            pltpu.VMEM((seq_n, slots, kv_width // 2), bf16),
            pltpu.VMEM((seq_n, slots, kv_width // 2), bf16),
            pltpu.VMEM((seq_n, slots, kv_width // 2), bf16),
            pltpu.VMEM((8, rows), jnp.int32),
            pltpu.VMEM((kvn, top, group * rows), jnp.int32),
            pltpu.VMEM((kvn, top, group * rows), jnp.float32),
            pltpu.VMEM((seq_n, slots, rows), bf16),
            pltpu.VMEM((kvn, group * rows, HEAD_DIM), bf16),
            pltpu.VMEM((2 * kvn, (SPAN + 1) * rows, HEAD_DIM), bf16),
            pltpu.VMEM(columns.shape, bf16),
            pltpu.VMEM((seq_n, 8, rows), jnp.int32),
            pltpu.VMEM((kvn, rows, HEAD_DIM), jnp.float32),
            pltpu.VMEM((SPAN, kvn, rows, HEAD_DIM), bf16),
            pltpu.VMEM((SPAN, kvn, rows, HEAD_DIM), bf16),
            pltpu.VMEM((seq_n, rows, dp_n * depth), bf16),
            pltpu.VMEM((seq_n, rows, kv_width), bf16),
            pltpu.VMEM((dp_n, depth, kv_width), link),
            pltpu.VMEM((dp_n, depth, kv_width), link),
        ] + [dma(shape) for shape in semaphores],
        compiler_params=pltpu.CompilerParams(
            collective_id=0, has_side_effects=True, vmem_limit_bytes=VMEM_BYTES
        ),
    )(
        weight_in, hidden, queries, values, row_target[None, :], cos_row, sin_row, columns,
        teacher_pick, teacher_prob, lower, cos_pos, sin_pos,
    )
    return attn_out, loss[0], weight_grad


def solution(mesh):
    both = P(("dp", "seq"), None)
    flat = P(("dp", "seq"))
    return jax.shard_map(
        local,
        mesh=mesh,
        in_specs=(both, both, both, flat, both, P("dp", None), both, both),
        out_specs=(both, flat, both),
        check_vma=False,
    )
```
